32 devices in a mesh: grp: 4 (over y, x), dom: 8 (over z, core).
Axes of the slice: x: 2, y: 2, z: 4, core: 2. Of those that a mesh axis runs over, the one named last changes fastest.
Arguments:
- table: float32 [131072, 256], P(('grp', 'dom')), may hold values from -6 to 6
- accum: float32 [131072], P(('grp', 'dom')), may hold values from 1e-07 to 0.0001
- w_self1: bfloat16 [256, 1024], replicated, may hold values from -0.375 to 0.375
- w_nbr1: bfloat16 [256, 1024], replicated, may hold values from -0.375 to 0.375
- w_self2: bfloat16 [1024, 1024], replicated, may hold values from -0.1875 to 0.1875
- w_nbr2: bfloat16 [1024, 1024], replicated, may hold values from -0.1875 to 0.1875
- fetch_owner: int32 [32768, 1], P(('grp', 'dom')), may hold values from 0 to 31; in each aligned block of 1024 rows (0 to 1023, 1024 to 2047, ...) at most 64 rows name the same one
- fetch_row: int32 [32768], P(('grp', 'dom')), may hold values from 0 to 4095
- self_slot: int32 [32768], P(('grp', 'dom')), may hold values from 0 to 1023
- nbr_one: int32 [32768, 8], P(('grp', 'dom')), may hold values from 0 to 1023
- nbr_two: int32 [32768, 8], P(('grp', 'dom')), may hold values from 0 to 1151
- cotangent: float32 [32768, 1024], P(('grp', 'dom')), may hold values from -0.06 to 0.06
Outputs:
- embedded: bfloat16 [32768, 1024], P(('grp', 'dom'))
- new_table: float32 [131072, 256], P(('grp', 'dom'))
- new_accum: float32 [131072], P(('grp', 'dom'))
- grad_self1: bfloat16 [256, 1024], replicated
- grad_nbr1: bfloat16 [256, 1024], replicated
- grad_self2: bfloat16 [1024, 1024], replicated
- grad_nbr2: bfloat16 [1024, 1024], replicated
The draws below stay inside these ranges and needn't reach their ends.
Inputs may be any that keep to these rules, and one draw needn't show every extreme that they name: `fetch_owner`: among the 1024 requests of one partition at most 64 name the same owner, and in some partition one owner is named exactly 64 times.
All inputs are finite; a program needn't handle non-finite values.
Results may differ from the reference program's by a relative error of at most 0.0045.
The reference program's roundings to bfloat16 on the way count: a program that leaves them out, or rounds other values in their place, can miss the bound.
Values may be sent and summed in bfloat16 or wider, within the bound.
A program may use at most 128 MiB of HBM per device.

```python
import math
import jax
import jax.numpy as jnp
import numpy as np
from jax import lax

EMB = 256
HID = 1024
FANOUT = 8
BORDER = 64
FETCH = 1024
NODES = 1024
ROWS_DEV = 4096
CAP = 64
ROWS = 131072
FETCH_ALL = 32768
TOKENS = 32768
N_GRP = 4
N_DOM = 8
DEVICES = 32


def plant(result, stream_key, low, top_value):
    longest = result.shape.index(max(result.shape))
    spots = []
    for shift in (0, 1):
        where = [jax.random.randint(jax.random.fold_in(stream_key, axis), (), 0, length) for axis, length in enumerate(result.shape)]
        where[longest] = (where[longest] + shift) % result.shape[longest]
        spots.append(tuple(where))
    return result.at[spots[0]].set(low).at[spots[1]].set(top_value)


def block_levels(stream_key, shape, pieces, least, top_value):
    level = 1.0
    for axis_at, blocks in pieces:
        steps = jax.random.uniform(jax.random.fold_in(jax.random.fold_in(stream_key, 6), axis_at), (blocks,), jnp.float32, least / len(pieces), top_value / len(pieces))
        level = level * jnp.repeat(jnp.exp(steps), shape[axis_at] // blocks).reshape((-1,) + (1,) * (len(shape) - 1 - axis_at))
    return level


def routed_block(stream_key, own, number, rows, count, top, most, slope):
    sequence = jax.random.permutation(stream_key, count)
    packed, ordinary = shares(count, rows * top, most, slope, True), shares(count, rows * top, most, slope, False)
    places = jnp.arange(count)

    def named(tallies, offset_by):
        used = int((tallies > 0).sum())
        fixed = max(1, used // 4)
        shifted = fixed + (places - fixed + offset_by * (used - fixed)) % max(1, count - fixed)
        return jnp.zeros((count,), jnp.int32).at[sequence[jnp.where(places < fixed, places, shifted)]].set(jnp.asarray(tallies, jnp.int32))

    tallies = jnp.where(number % 4 == 0, named(packed, number // 4), named(ordinary, number - number // 4 - 1))
    mixed = jax.random.permutation(jax.random.fold_in(own, 3), count)
    giver, taker = mixed[0:count // 2 * 2:2], mixed[1:count // 2 * 2:2]
    room = jnp.minimum(tallies[giver] - 1, most - tallies[taker]) // 2
    room = jnp.where((giver == sequence[0]) | (taker == sequence[0]) | (tallies[taker] == 0), 0, jnp.maximum(room, 0))
    shifted = jax.random.randint(jax.random.fold_in(own, 4), (count // 2,), 0, 1 << 20) % (room + 1)
    tallies = tallies.at[giver].add(-shifted).at[taker].add(shifted)
    members = jnp.searchsorted(jnp.cumsum(tallies), jnp.arange(rows * top), side="right").astype(jnp.int32)
    grid = members.reshape(top, rows).T
    grid = grid[jax.random.permutation(jax.random.fold_in(own, 1), rows)]
    offset_by = jax.random.randint(jax.random.fold_in(own, 2), (rows, 1), 0, top)
    return jnp.take_along_axis(grid, (jnp.arange(top)[None, :] + offset_by) % top, axis=1)


def shares(count, total, most, lean, full):
    weights = [(1 << 20) // math.isqrt(standing ** lean) + 1 for standing in range(1, count + 1)]
    largest = most if full else min(most, max(-(-total // count), total * weights[0] // sum(weights)))
    least = 1 if total - largest >= count - 1 else 0
    given, surplus = [largest] + [least] * (count - 1), total - largest - least * (count - 1)
    while surplus > 0:
        movable = [i for i in range(1, count) if given[i] < largest] or [i for i in range(1, count) if given[i] < most]
        pool, left = sum([weights[i] for i in movable]), surplus
        for i in movable:
            more = min(most - given[i], max(1, left * weights[i] // pool), surplus)
            given[i] = given[i] + more
            surplus = surplus - more
    return np.array(given)


def scatter_about(own_key, extent, scale, most, split=(), held_as=jnp.bfloat16):
    entries = scale * jax.random.normal(own_key, extent, jnp.float32)
    if split:
        entries = entries * block_levels(own_key, extent, split, -0.22, 0.18)
    return jnp.clip(entries, -most, most).astype(held_as)


def setup_inputs(seed: int = 0) -> dict:
    key_list = jax.random.split(jax.random.key(seed), 13)
    table = scatter_about(key_list[0], (ROWS, EMB), 1.0, 6.0, ((0, 32),), jnp.float32)
    accum = jnp.clip(jnp.exp(math.log(0.0001) - 6.9077552 * jax.random.uniform(key_list[1], (ROWS,), jnp.float32) ** block_levels(key_list[1], (ROWS,), ((0, 32),), -0.2, 0.2)), 1.0000000116860974e-07, 0.0001)
    w_self1 = scatter_about(key_list[2], (EMB, HID), EMB ** -0.5, 0.375)
    w_nbr1 = scatter_about(key_list[3], (EMB, HID), EMB ** -0.5, 0.375)
    w_self2 = scatter_about(key_list[4], (HID, HID), HID ** -0.5, 0.1875)
    w_nbr2 = scatter_about(key_list[5], (HID, HID), HID ** -0.5, 0.1875)
    fetch_owner_keys = jax.random.split(jax.random.fold_in(key_list[6], 1), FETCH_ALL // FETCH)
    fetch_owner_turns = jax.random.permutation(jax.random.fold_in(key_list[6], 3), FETCH_ALL // FETCH)
    fetch_owner = jax.vmap(lambda own, number: routed_block(jax.random.fold_in(key_list[6], 2), own, number, FETCH, DEVICES, 1, CAP, 2))(fetch_owner_keys, fetch_owner_turns).reshape((FETCH_ALL, 1))
    fetch_row = plant(jax.random.randint(key_list[7], (FETCH_ALL,), 0, ROWS_DEV), jax.random.fold_in(key_list[7], 1), 0, ROWS_DEV - 1).astype(jnp.int32)
    self_slot = plant(jax.random.randint(key_list[8], (TOKENS,), 0, FETCH), jax.random.fold_in(key_list[8], 1), 0, FETCH - 1).astype(jnp.int32)
    nbr_one = plant(jax.random.randint(key_list[9], (TOKENS, FANOUT), 0, FETCH), jax.random.fold_in(key_list[9], 1), 0, FETCH - 1).astype(jnp.int32)
    nbr_two = plant(jax.random.randint(key_list[10], (TOKENS, FANOUT), 0, NODES + 2 * BORDER), jax.random.fold_in(key_list[10], 1), 0, (NODES + 2 * BORDER) - 1).astype(jnp.int32)
    cotangent = scatter_about(key_list[11], (TOKENS, HID), 0.01, 0.06, ((0, 32),), jnp.float32)
    return {"table": table, "accum": accum, "w_self1": w_self1, "w_nbr1": w_nbr1, "w_self2": w_self2, "w_nbr2": w_nbr2, "fetch_owner": fetch_owner, "fetch_row": fetch_row, "self_slot": self_slot, "nbr_one": nbr_one, "nbr_two": nbr_two, "cotangent": cotangent}


epsilon = 1e-06
learning_rate = 0.1

def swish_slope(values):
    logistic = jax.nn.sigmoid(values)
    return logistic + values * logistic * (1.0 - logistic)

def counts(neighbours, widths):
    hits = (neighbours[:, :, None] == jnp.arange(widths, dtype=jnp.int32)[None, None, :]).astype(jnp.float32)
    return lax.optimization_barrier(jnp.sum(hits, axis=1)).astype(jnp.bfloat16)

def contract_rows(left, right):
    return lax.dot_general(left, right, (((0,), (0,)), ((), ())), preferred_element_type=jnp.float32)

def contract_cols(left, right):
    return lax.dot_general(left, right, (((1,), (1,)), ((), ())), preferred_element_type=jnp.float32)

def forward_one(fetched, slot_index, neighbours, w_self1, w_nbr1):
    fanout = neighbours.shape[1]
    self_rows = fetched[slot_index]
    adjacency_one = counts(neighbours, fetched.shape[0])
    pooled_one = (jnp.dot(adjacency_one, fetched, preferred_element_type=jnp.float32) / fanout).astype(jnp.bfloat16)
    before_one = jnp.dot(self_rows, w_self1, preferred_element_type=jnp.float32) + jnp.dot(pooled_one, w_nbr1, preferred_element_type=jnp.float32)
    return (self_rows, adjacency_one, pooled_one, before_one)

def forward_two(hidden_one, bordered, neighbours, w_self2, w_nbr2):
    fanout = neighbours.shape[1]
    adjacency_two = counts(neighbours, bordered.shape[0])
    pooled_two = (jnp.dot(adjacency_two, bordered, preferred_element_type=jnp.float32) / fanout).astype(jnp.bfloat16)
    before_two = jnp.dot(hidden_one, w_self2, preferred_element_type=jnp.float32) + jnp.dot(pooled_two, w_nbr2, preferred_element_type=jnp.float32)
    lifted = jax.nn.silu(before_two)
    scale = lax.rsqrt(lax.optimization_barrier(jnp.mean(lifted * lifted, axis=1, keepdims=True)) + epsilon)
    return (adjacency_two, pooled_two, before_two, lifted * scale, scale)

def backward_two(upstream, hidden_one, adjacency_two, pooled_two, before_two, normed, scale, w_self2, w_nbr2):
    fanout_inv = 1.0 / FANOUT
    grad_lifted = scale * (upstream - normed * lax.optimization_barrier(jnp.mean(upstream * normed, axis=1, keepdims=True)))
    grad_before = (grad_lifted * swish_slope(before_two)).astype(jnp.bfloat16)
    g_self2 = contract_rows(hidden_one, grad_before)
    g_nbr2 = contract_rows(pooled_two, grad_before)
    grad_hidden = contract_cols(grad_before, w_self2)
    grad_pooled = contract_cols(grad_before, w_nbr2).astype(jnp.bfloat16)
    grad_bordered = contract_rows(adjacency_two, grad_pooled) * fanout_inv
    return (g_self2, g_nbr2, grad_hidden, grad_bordered)

def backward_one(grad_hidden, before_one, self_rows, adjacency_one, pooled_one, slot_index, w_self1, w_nbr1):
    fanout_inv = 1.0 / FANOUT
    grad_before = (grad_hidden * swish_slope(before_one)).astype(jnp.bfloat16)
    g_self1 = contract_rows(self_rows, grad_before)
    g_nbr1 = contract_rows(pooled_one, grad_before)
    grad_self_rows = contract_cols(grad_before, w_self1)
    grad_pooled = contract_cols(grad_before, w_nbr1).astype(jnp.bfloat16)
    grad_fetched = jax.ops.segment_sum(grad_self_rows, slot_index, num_segments=adjacency_one.shape[1])
    grad_fetched = grad_fetched + contract_rows(adjacency_one, grad_pooled) * fanout_inv
    return (g_self1, g_nbr1, grad_fetched)

def reference(table, accum, w_self1, w_nbr1, w_self2, w_nbr2, fetch_owner, fetch_row, self_slot, nbr_one, nbr_two, cotangent):
    parts = N_GRP * N_DOM
    global_rows = (fetch_owner[:, 0] * ROWS_DEV + fetch_row).astype(jnp.int32)
    fetched = table[global_rows].astype(jnp.bfloat16).reshape(parts, FETCH, EMB)
    slots = self_slot.reshape(parts, NODES)
    first_lists = nbr_one.reshape(parts, NODES, FANOUT)
    second_lists = nbr_two.reshape(parts, NODES, FANOUT)
    upstream_all = cotangent.reshape(parts, NODES, HID)

    def hidden_of(inputs):
        rows, slot_index, lists = inputs
        outcome = forward_one(rows, slot_index, lists, w_self1, w_nbr1)
        return jax.nn.silu(outcome[3]).astype(jnp.bfloat16)
    hidden_one = lax.map(hidden_of, (fetched, slots, first_lists))
    bordered = jnp.concatenate([jnp.roll(hidden_one, 1, axis=0)[:, NODES - BORDER:], hidden_one, jnp.roll(hidden_one, -1, axis=0)[:, :BORDER]], axis=1)

    def second_step(carry, inputs):
        hidden, bordered_rows, lists, upstream = inputs
        adjacency_two, pooled_two, before_two, normed, scale = forward_two(hidden, bordered_rows, lists, w_self2, w_nbr2)
        g_self2, g_nbr2, grad_hidden, grad_bordered = backward_two(upstream, hidden, adjacency_two, pooled_two, before_two, normed, scale, w_self2, w_nbr2)
        middle = grad_hidden + grad_bordered[BORDER:BORDER + NODES]
        edges = jnp.concatenate([grad_bordered[:BORDER], grad_bordered[BORDER + NODES:]], axis=0)
        return ((carry[0] + g_self2, carry[1] + g_nbr2), (normed.astype(jnp.bfloat16), middle, edges))
    zero_hh = jnp.zeros((HID, HID), jnp.float32)
    (sum_self2, sum_nbr2), (embedded, middle, edges) = lax.scan(second_step, (zero_hh, zero_hh), (hidden_one, bordered, second_lists, upstream_all))
    from_before = jnp.roll(edges, 1, axis=0)[:, BORDER:]
    from_after = jnp.roll(edges, -1, axis=0)[:, :BORDER]
    grad_hidden_all = middle.at[:, :BORDER].add(from_before).at[:, NODES - BORDER:].add(from_after)

    def first_step(carry, inputs):
        rows, slot_index, lists, grad_hidden = inputs
        self_rows, adjacency_one, pooled_one, before_one = forward_one(rows, slot_index, lists, w_self1, w_nbr1)
        g_self1, g_nbr1, grad_fetched = backward_one(grad_hidden, before_one, self_rows, adjacency_one, pooled_one, slot_index, w_self1, w_nbr1)
        return ((carry[0] + g_self1, carry[1] + g_nbr1), grad_fetched)
    zero_eh = jnp.zeros((EMB, HID), jnp.float32)
    (sum_self1, sum_nbr1), grad_fetched = lax.scan(first_step, (zero_eh, zero_eh), (fetched, slots, first_lists, grad_hidden_all))
    row_grads = jax.ops.segment_sum(grad_fetched.reshape(-1, EMB), global_rows, num_segments=ROWS_DEV * N_GRP * N_DOM)
    new_accum = accum + lax.optimization_barrier(jnp.mean(row_grads * row_grads, axis=1))
    new_table = table - learning_rate * row_grads / (jnp.sqrt(new_accum)[:, None] + epsilon)
    return (embedded.reshape(-1, HID), new_table, new_accum, sum_self1.astype(jnp.bfloat16), sum_nbr1.astype(jnp.bfloat16), sum_self2.astype(jnp.bfloat16), sum_nbr2.astype(jnp.bfloat16))
```

```python
import functools

import jax
import jax.numpy as jnp
from jax import lax
from jax.experimental import pallas as pl
from jax.experimental.pallas import tpu as pltpu
from jax.sharding import PartitionSpec as P

FANOUT = 8
BORDER = 64


epsilon = 1e-06
learning_rate = 0.1


def with_halo(x, sides, width):
    for axis, dim in sides:
        devices, length = (lax.axis_size(axis), x.shape[dim])
        up = [(i, (i + 1) % devices) for i in range(devices)]
        down = [(j, i) for i, j in up]
        last = lax.slice_in_dim(x, length - width, length, axis=dim)
        leading = lax.slice_in_dim(x, 0, width, axis=dim)
        before = lax.ppermute(last, axis, up)
        after = lax.ppermute(leading, axis, down)
        x = jnp.concatenate([before, x, after], axis=dim)
    return x


def swish_slope(values):
    logistic = jax.nn.sigmoid(values)
    return logistic + values * logistic * (1.0 - logistic)


def hot(index, width):
    return (index[:, None] == jnp.arange(width, dtype=jnp.int32)[None, :]).astype(jnp.bfloat16)


def counts(neighbours, widths):
    lanes = jnp.arange(widths, dtype=jnp.int32)[None, :]
    total = jnp.zeros((neighbours.shape[0], widths), jnp.float32)
    for k in range(neighbours.shape[1]):
        total = total + (neighbours[:, k : k + 1] == lanes).astype(jnp.float32)
    return total.astype(jnp.bfloat16)


def contract_rows(left, right):
    return lax.dot_general(
        left, right, (((0,), (0,)), ((), ())), preferred_element_type=jnp.float32
    )


def contract_cols(left, right):
    return lax.dot_general(
        left, right, (((1,), (1,)), ((), ())), preferred_element_type=jnp.float32
    )


def forward_one(fetched, slot_hot, neighbours, w_self1, w_nbr1):
    fanout = neighbours.shape[1]
    self_rows = jnp.dot(
        slot_hot, fetched, preferred_element_type=jnp.float32
    ).astype(jnp.bfloat16)
    adjacency_one = counts(neighbours, fetched.shape[0])
    pooled_one = (
        jnp.dot(adjacency_one, fetched, preferred_element_type=jnp.float32) / fanout
    ).astype(jnp.bfloat16)
    before_one = jnp.dot(self_rows, w_self1, preferred_element_type=jnp.float32) + jnp.dot(
        pooled_one, w_nbr1, preferred_element_type=jnp.float32
    )
    return (self_rows, adjacency_one, pooled_one, before_one)


def forward_two(hidden_one, bordered, neighbours, w_self2, w_nbr2):
    fanout = neighbours.shape[1]
    adjacency_two = counts(neighbours, bordered.shape[0])
    pooled_two = (
        jnp.dot(adjacency_two, bordered, preferred_element_type=jnp.float32) / fanout
    ).astype(jnp.bfloat16)
    before_two = jnp.dot(hidden_one, w_self2, preferred_element_type=jnp.float32) + jnp.dot(
        pooled_two, w_nbr2, preferred_element_type=jnp.float32
    )
    lifted = jax.nn.silu(before_two)
    scale = lax.rsqrt(jnp.mean(lifted * lifted, axis=1, keepdims=True) + epsilon)
    return (adjacency_two, pooled_two, before_two, lifted * scale, scale)


def backward_two(
    upstream, hidden_one, adjacency_two, pooled_two, before_two, normed, scale, w_self2, w_nbr2
):
    fanout_inv = 1.0 / FANOUT
    grad_lifted = scale * (upstream - normed * jnp.mean(upstream * normed, axis=1, keepdims=True))
    grad_before = (grad_lifted * swish_slope(before_two)).astype(jnp.bfloat16)
    g_self2 = contract_rows(hidden_one, grad_before)
    g_nbr2 = contract_rows(pooled_two, grad_before)
    grad_hidden = contract_cols(grad_before, w_self2)
    grad_pooled = contract_cols(grad_before, w_nbr2).astype(jnp.bfloat16)
    grad_bordered = contract_rows(adjacency_two, grad_pooled) * fanout_inv
    return (g_self2, g_nbr2, grad_hidden, grad_bordered)


def backward_one(
    grad_hidden, before_one, self_rows, adjacency_one, pooled_one, slot_hot, w_self1, w_nbr1
):
    fanout_inv = 1.0 / FANOUT
    grad_before = (grad_hidden * swish_slope(before_one)).astype(jnp.bfloat16)
    g_self1 = contract_rows(self_rows, grad_before)
    g_nbr1 = contract_rows(pooled_one, grad_before)
    grad_self_rows = contract_cols(grad_before, w_self1)
    grad_pooled = contract_cols(grad_before, w_nbr1).astype(jnp.bfloat16)
    upper = grad_self_rows.astype(jnp.bfloat16)
    lower = (grad_self_rows - upper.astype(jnp.float32)).astype(jnp.bfloat16)
    width = upper.shape[1]
    both = contract_rows(slot_hot, jnp.concatenate([upper, lower], axis=1))
    grad_fetched = both[:, :width] + both[:, width:] + contract_rows(adjacency_one, grad_pooled) * fanout_inv
    return (g_self1, g_nbr1, grad_fetched)


def trade_requests(wanted):
    return lax.all_to_all(wanted, ("grp", "dom"), split_axis=0, concat_axis=0, tiled=True)


def trade_rows(found):
    return lax.all_to_all(found, ("grp", "dom"), split_axis=0, concat_axis=0, tiled=True)


def trade_grads(partial_grads):
    return lax.all_to_all(partial_grads, ("grp", "dom"), split_axis=0, concat_axis=0, tiled=True)


def tile_of(length, most):
    return most if length % most == 0 else length


def pick_kernel(index_ref, table_ref, found_ref, rounded):
    @pl.when(pl.program_id(0) == 0)
    def _():
        rounded[...] = table_ref[...].astype(jnp.bfloat16)

    lanes = lax.broadcasted_iota(jnp.int32, (index_ref.shape[0], table_ref.shape[0]), 1)
    chosen = jnp.where(index_ref[...] == lanes, 1.0, 0.0).astype(jnp.bfloat16)
    found_ref[...] = jnp.dot(chosen, rounded[...], preferred_element_type=jnp.float32).astype(
        jnp.bfloat16
    )


def pick_rows(index, table):
    count, (rows, width) = index.shape[0], table.shape
    tile = tile_of(count, 256)
    return pl.pallas_call(
        pick_kernel,
        grid=(count // tile,),
        out_shape=jax.ShapeDtypeStruct((count, width), jnp.bfloat16),
        in_specs=[
            pl.BlockSpec((tile, 1), lambda i: (i, 0)),
            pl.BlockSpec((rows, width), lambda i: (0, 0)),
        ],
        out_specs=pl.BlockSpec((tile, width), lambda i: (i, 0)),
        scratch_shapes=[pltpu.VMEM((rows, width), jnp.bfloat16)],
        compiler_params=pltpu.CompilerParams(vmem_limit_bytes=48 * 2**20),
        cost_estimate=pl.CostEstimate(
            flops=2 * count * rows * width, bytes_accessed=rows * width * 4, transcendentals=0
        ),
    )(index, table)


def update_kernel(index_ref, grads_ref, table_ref, accum_ref, new_table_ref, new_accum_ref):
    rows, width = table_ref.shape
    start = pl.program_id(0) * rows
    numbers = start + lax.broadcasted_iota(jnp.int32, (rows, index_ref.shape[1]), 0)
    chosen = jnp.where(index_ref[...] == numbers, 1.0, 0.0).astype(jnp.bfloat16)
    grads = jnp.dot(chosen, grads_ref[...], preferred_element_type=jnp.float32)
    level = accum_ref[...] + jnp.mean(grads * grads, axis=1, keepdims=True)
    new_accum_ref[...] = level
    new_table_ref[...] = table_ref[...] - learning_rate * grads / (jnp.sqrt(level) + epsilon)


def update_rows(index, grads, table, accum):
    count, (rows, width) = index.shape[1], table.shape
    tile = tile_of(rows, 512)
    by_tile = lambda i: (i, 0)
    whole = lambda i: (0, 0)
    return pl.pallas_call(
        update_kernel,
        grid=(rows // tile,),
        out_shape=(
            jax.ShapeDtypeStruct((rows, width), jnp.float32),
            jax.ShapeDtypeStruct((rows, 1), jnp.float32),
        ),
        in_specs=[
            pl.BlockSpec((1, count), whole),
            pl.BlockSpec((count, width), whole),
            pl.BlockSpec((tile, width), by_tile),
            pl.BlockSpec((tile, 1), by_tile),
        ],
        out_specs=(pl.BlockSpec((tile, width), by_tile), pl.BlockSpec((tile, 1), by_tile)),
        compiler_params=pltpu.CompilerParams(vmem_limit_bytes=48 * 2**20),
        cost_estimate=pl.CostEstimate(
            flops=2 * count * rows * width, bytes_accessed=rows * width * 8, transcendentals=0
        ),
    )(index, grads, table, accum)


def reduce_kernel(
    groups,
    domains,
    chunks,
    x_ref,
    out_ref,
    acc,
    core_out,
    core_in,
    half_out,
    half_in,
    z_out,
    z_in,
    core_sem,
    half_sem,
    z_sem,
):
    grp, dom = lax.axis_index("grp"), lax.axis_index("dom")
    core, layer = dom % 2, dom // 2
    layers = domains // 2
    bits = groups.bit_length() - 1
    half = groups * layers

    def other_grp(bit):
        mine = (grp // 2**bit) % 2
        return grp + (1 - 2 * mine) * 2**bit

    core_id = (grp, dom + 1 - 2 * core)
    half_ids = [(other_grp(bit), dom) for bit in range(bits)]
    layer_ids = [(grp, ((layer + d) % layers) * 2 + core) for d in range(1, layers)]
    everyone = [core_id] + half_ids + layer_ids
    barrier = pltpu.get_barrier_semaphore()
    for target in everyone:
        pl.semaphore_signal(
            barrier, inc=1, device_id=target, device_id_type=pl.DeviceIdType.MESH
        )
    pl.semaphore_wait(barrier, len(everyone))

    def send(source, target_ref, sems, target):
        copy = pltpu.make_async_remote_copy(
            src_ref=source,
            dst_ref=target_ref,
            send_sem=sems.at[0],
            recv_sem=sems.at[1],
            device_id=target,
            device_id_type=pl.DeviceIdType.MESH,
        )
        copy.start()
        return copy

    def each(count, body):
        def step(i, carry):
            body(i)
            return carry

        lax.fori_loop(0, count, step, 0)

    orders = [
        list(range(bits)) if k % 2 == 0 else list(range(bits))[::-1] for k in range(chunks)
    ]
    bit_of = lambda bit: (grp // 2**bit) % 2
    sent = []
    starts = []
    for k in range(chunks):
        at, size = core * half, half
        places = [at]
        for bit in orders[k]:
            size //= 2
            at = at + bit_of(bit) * size
            places.append(at)
        starts.append(places)

    def offset_of(step):
        return sum(half >> (i + 1) for i in range(step))

    copies = []
    for k in range(chunks):

        def narrow(i, k=k):
            core_out[k, i] = x_ref[k, (1 - core) * half + i].astype(jnp.bfloat16)

        each(half, narrow)
        copies.append(send(core_out.at[k], core_in.at[k], core_sem.at[0, k], core_id))
    sent += copies

    for step in range(bits):
        later = []
        size = half >> (step + 1)
        slots = pl.ds(offset_of(step), size)
        for k in range(chunks):
            bit = orders[k][step]
            mine = bit_of(bit)
            base = starts[k][step] - starts[k][0]
            keep = base + mine * size
            give = base + (1 - mine) * size
            copies[k].wait_recv()

            def total(i, at, k=k, step=step):
                if step == 0:
                    return x_ref[k, core * half + at + i] + core_in[k, at + i].astype(jnp.float32)
                arrived = offset_of(step - 1) + at + i - base
                return acc[k, at + i] + half_in[k, arrived].astype(jnp.float32)

            def give_part(i, k=k, give=give, total=total, step=step):
                half_out[k, offset_of(step) + i] = total(i, give).astype(jnp.bfloat16)

            each(size, give_part)
            later.append(
                send(
                    half_out.at[k, slots],
                    half_in.at[k, slots],
                    half_sem.at[0, step, k],
                    half_ids[bit],
                )
            )

            def keep_part(i, k=k, keep=keep, total=total):
                acc[k, keep + i] = total(i, keep)

            each(size, keep_part)
        copies = later
        sent += copies

    z_copies = []
    for k in range(chunks):
        base = starts[k][bits] - starts[k][0]
        copies[k].wait_recv()
        last = offset_of(bits - 1)
        mine_now = []
        for d in range(1, layers):
            at = (layer + d) % layers
            z_out[k, d - 1] = (
                acc[k, base + at] + half_in[k, last + at].astype(jnp.float32)
            ).astype(jnp.bfloat16)
            mine_now.append(
                send(
                    z_out.at[k, d - 1],
                    z_in.at[k, d - 1],
                    z_sem.at[0, k, d - 1],
                    layer_ids[d - 1],
                )
            )
        z_copies.append(mine_now)
        sent += mine_now

    gathers = []
    for k in range(chunks):
        base = starts[k][bits] - starts[k][0]
        last = offset_of(bits - 1)
        value = acc[k, base + layer] + half_in[k, last + layer].astype(jnp.float32)
        for copy in z_copies[k]:
            copy.wait_recv()
        for d in range(1, layers):
            value = value + z_in[k, d - 1].astype(jnp.float32)
        at = starts[k][bits] + layer
        out_ref[k, at] = value.astype(jnp.bfloat16)
        mine_now = []
        for d in range(1, layers):
            mine_now.append(
                send(out_ref.at[k, at], out_ref.at[k, at], z_sem.at[1, k, d - 1], layer_ids[d - 1])
            )
        gathers.append(mine_now)
        sent += mine_now

    for step in reversed(range(bits)):
        later = []
        size = half >> (step + 1)
        for k in range(chunks):
            for copy in gathers[k]:
                copy.wait_recv()
            mine = pl.ds(starts[k][step + 1], size)
            later.append(
                [
                    send(
                        out_ref.at[k, mine],
                        out_ref.at[k, mine],
                        half_sem.at[1, step, k],
                        half_ids[orders[k][step]],
                    )
                ]
            )
            sent += later[-1]
        gathers = later
    last_copies = []
    for k in range(chunks):
        for copy in gathers[k]:
            copy.wait_recv()
        mine = pl.ds(starts[k][0], half)
        last_copies.append(
            send(out_ref.at[k, mine], out_ref.at[k, mine], core_sem.at[1, k], core_id)
        )
    for copy in last_copies:
        copy.wait_recv()
    for copy in sent + last_copies:
        copy.wait_send()


def sum_all(g_self1, g_nbr1, g_self2, g_nbr2, groups, domains):
    devices = groups * domains
    layers = domains // 2
    bits = groups.bit_length() - 1
    stacked = jnp.concatenate([g_self2, g_nbr2, g_self1, g_nbr1], axis=0)
    part = g_self1.shape[0] + g_nbr1.shape[0]
    chunks = stacked.shape[0] // part
    piece = 16
    width = part * stacked.shape[1] // (devices * piece)
    half = devices // 2
    x = stacked.reshape(chunks, devices, piece, width)
    unit = (piece, width)
    total = pl.pallas_call(
        functools.partial(reduce_kernel, groups, domains, chunks),
        out_shape=jax.ShapeDtypeStruct((chunks, devices) + unit, jnp.bfloat16),
        in_specs=[pl.BlockSpec(memory_space=pltpu.VMEM)],
        out_specs=pl.BlockSpec(memory_space=pltpu.VMEM),
        scratch_shapes=[
            pltpu.VMEM((chunks, half) + unit, jnp.float32),
            pltpu.VMEM((chunks, half) + unit, jnp.bfloat16),
            pltpu.VMEM((chunks, half) + unit, jnp.bfloat16),
            pltpu.VMEM((chunks, half) + unit, jnp.bfloat16),
            pltpu.VMEM((chunks, half) + unit, jnp.bfloat16),
            pltpu.VMEM((chunks, layers) + unit, jnp.bfloat16),
            pltpu.VMEM((chunks, layers) + unit, jnp.bfloat16),
            pltpu.SemaphoreType.DMA((2, chunks, 2)),
            pltpu.SemaphoreType.DMA((2, bits, chunks, 2)),
            pltpu.SemaphoreType.DMA((2, chunks, layers, 2)),
        ],
        compiler_params=pltpu.CompilerParams(
            collective_id=0, has_side_effects=True, vmem_limit_bytes=56 * 2**20
        ),
        cost_estimate=pl.CostEstimate(
            flops=4 * stacked.size, bytes_accessed=6 * stacked.size, transcendentals=0
        ),
    )(x)
    total = total.reshape(stacked.shape)
    big, small = g_self2.shape[0], g_self1.shape[0]
    return (
        total[2 * big : 2 * big + small],
        total[2 * big + small :],
        total[:big],
        total[big : 2 * big],
    )


def local(
    table,
    accum,
    w_self1,
    w_nbr1,
    w_self2,
    w_nbr2,
    fetch_owner,
    fetch_row,
    self_slot,
    nbr_one,
    nbr_two,
    cotangent,
):
    groups = lax.axis_size("grp")
    domains = lax.axis_size("dom")
    devices = groups * domains
    fetch_count = fetch_row.shape[0]
    capacity = max(2, 2 * fetch_count // devices)
    emb_width = table.shape[1]
    owners = fetch_owner[:, 0]
    owner_hot = hot(owners, devices)
    order = jnp.arange(fetch_count, dtype=jnp.int32)
    earlier = (order[:, None] > order[None, :]).astype(jnp.bfloat16)
    before = jnp.dot(earlier, owner_hot, preferred_element_type=jnp.float32)
    ranks = jnp.sum(before * owner_hot.astype(jnp.float32), axis=1).astype(jnp.int32)
    position = owners * capacity + ranks
    rank_hot = hot(ranks, capacity)
    digits = jnp.concatenate(
        [
            rank_hot * (fetch_row // 128).astype(jnp.bfloat16)[:, None],
            rank_hot * (fetch_row % 128).astype(jnp.bfloat16)[:, None],
        ],
        axis=1,
    )
    digits = contract_rows(owner_hot, digits)
    wanted = (digits[:, :capacity] * 128.0 + digits[:, capacity:]).astype(jnp.int32)
    place_hot = hot(position, devices * capacity)
    slot_hot = hot(self_slot, fetch_count)
    incoming = trade_requests(wanted)
    found = pick_rows(incoming.reshape(-1, 1), table).reshape(devices, capacity, emb_width)
    replies = trade_rows(found)
    fetched = jnp.dot(
        place_hot,
        replies.reshape(devices * capacity, emb_width),
        preferred_element_type=jnp.float32,
    ).astype(jnp.bfloat16)
    self_rows, adjacency_one, pooled_one, before_one = forward_one(
        fetched, slot_hot, nbr_one, w_self1, w_nbr1
    )
    hidden_one = jax.nn.silu(before_one).astype(jnp.bfloat16)
    nodes = hidden_one.shape[0]
    bordered = with_halo(hidden_one, ((("grp", "dom"), 0),), BORDER)
    adjacency_two, pooled_two, before_two, normed, scale = forward_two(
        hidden_one, bordered, nbr_two, w_self2, w_nbr2
    )
    embedded = normed.astype(jnp.bfloat16)
    g_self2, g_nbr2, grad_hidden, grad_bordered = backward_two(
        cotangent, hidden_one, adjacency_two, pooled_two, before_two, normed, scale, w_self2, w_nbr2
    )
    middle = grad_hidden + grad_bordered[BORDER : BORDER + nodes]
    edges = jnp.concatenate([grad_bordered[:BORDER], grad_bordered[BORDER + nodes :]], axis=0)
    arrived = with_halo(edges, ((("grp", "dom"), 0),), BORDER)
    grad_hidden = (
        middle.at[:BORDER]
        .add(arrived[:BORDER])
        .at[nodes - BORDER :]
        .add(arrived[arrived.shape[0] - BORDER :])
    )
    g_self1, g_nbr1, grad_fetched = backward_one(
        grad_hidden, before_one, self_rows, adjacency_one, pooled_one, slot_hot, w_self1, w_nbr1
    )
    grad_buffer = (
        contract_rows(place_hot, grad_fetched.astype(jnp.bfloat16))
        .astype(jnp.bfloat16)
        .reshape(devices, capacity, emb_width)
    )
    returned = trade_grads(grad_buffer)
    sum_self1, sum_nbr1, sum_self2, sum_nbr2 = sum_all(
        g_self1, g_nbr1, g_self2, g_nbr2, groups, domains
    )
    new_table, new_accum = update_rows(
        incoming.reshape(1, -1), returned.reshape(-1, emb_width), table, accum.reshape(-1, 1)
    )
    new_accum = new_accum.reshape(-1)
    return (embedded, new_table, new_accum, sum_self1, sum_nbr1, sum_self2, sum_nbr2)


def solution(mesh):
    in_specs = (
        P(("grp", "dom"), None),
        P(("grp", "dom")),
        P(),
        P(),
        P(),
        P(),
        P(("grp", "dom"), None),
        P(("grp", "dom")),
        P(("grp", "dom")),
        P(("grp", "dom"), None),
        P(("grp", "dom"), None),
        P(("grp", "dom"), None),
    )
    out_specs = (
        P(("grp", "dom"), None),
        P(("grp", "dom"), None),
        P(("grp", "dom")),
        P(),
        P(),
        P(),
        P(),
    )
    return jax.shard_map(local, mesh=mesh, in_specs=in_specs, out_specs=out_specs, check_vma=False)
```

```python
import functools

import jax
import jax.numpy as jnp
from jax import lax
from jax.experimental import pallas as pl
from jax.experimental.pallas import tpu as pltpu
from jax.sharding import PartitionSpec as P

FANOUT = 8
BORDER = 64


epsilon = 1e-06
learning_rate = 0.1


def with_halo(x, sides, width):
    for axis, dim in sides:
        devices, length = (lax.axis_size(axis), x.shape[dim])
        up = [(i, (i + 1) % devices) for i in range(devices)]
        down = [(j, i) for i, j in up]
        last = lax.slice_in_dim(x, length - width, length, axis=dim)
        leading = lax.slice_in_dim(x, 0, width, axis=dim)
        before = lax.ppermute(last, axis, up)
        after = lax.ppermute(leading, axis, down)
        x = jnp.concatenate([before, x, after], axis=dim)
    return x


def swish_slope(values):
    logistic = jax.nn.sigmoid(values)
    return logistic + values * logistic * (1.0 - logistic)


def hot(index, width):
    return (index[:, None] == jnp.arange(width, dtype=jnp.int32)[None, :]).astype(jnp.bfloat16)


def counts(neighbours, widths):
    lanes = jnp.arange(widths, dtype=jnp.int32)[None, :]
    total = jnp.zeros((neighbours.shape[0], widths), jnp.float32)
    for k in range(neighbours.shape[1]):
        total = total + (neighbours[:, k : k + 1] == lanes).astype(jnp.float32)
    return lax.optimization_barrier(total.astype(jnp.bfloat16))


def contract_rows(left, right):
    return lax.dot_general(
        left, right, (((0,), (0,)), ((), ())), preferred_element_type=jnp.float32
    )


def contract_cols(left, right):
    return lax.dot_general(
        left, right, (((1,), (1,)), ((), ())), preferred_element_type=jnp.float32
    )


def forward_one(fetched, slot_hot, neighbours, w_self1, w_nbr1):
    fanout = neighbours.shape[1]
    self_rows = jnp.dot(
        slot_hot, fetched, preferred_element_type=jnp.float32
    ).astype(jnp.bfloat16)
    adjacency_one = counts(neighbours, fetched.shape[0])
    pooled_one = (
        jnp.dot(adjacency_one, fetched, preferred_element_type=jnp.float32) / fanout
    ).astype(jnp.bfloat16)
    before_one = jnp.dot(self_rows, w_self1, preferred_element_type=jnp.float32) + jnp.dot(
        pooled_one, w_nbr1, preferred_element_type=jnp.float32
    )
    return (self_rows, adjacency_one, pooled_one, before_one)


def forward_two(hidden_one, bordered, neighbours, w_self2, w_nbr2):
    fanout = neighbours.shape[1]
    adjacency_two = counts(neighbours, bordered.shape[0])
    pooled_two = (
        jnp.dot(adjacency_two, bordered, preferred_element_type=jnp.float32) / fanout
    ).astype(jnp.bfloat16)
    before_two = jnp.dot(hidden_one, w_self2, preferred_element_type=jnp.float32) + jnp.dot(
        pooled_two, w_nbr2, preferred_element_type=jnp.float32
    )
    lifted = jax.nn.silu(before_two)
    scale = lax.rsqrt(jnp.mean(lifted * lifted, axis=1, keepdims=True) + epsilon)
    return (adjacency_two, pooled_two, before_two, lifted * scale, scale)


def backward_two(
    upstream, hidden_one, adjacency_two, pooled_two, before_two, normed, scale, w_self2, w_nbr2
):
    fanout_inv = 1.0 / FANOUT
    grad_lifted = scale * (upstream - normed * jnp.mean(upstream * normed, axis=1, keepdims=True))
    grad_before = (grad_lifted * swish_slope(before_two)).astype(jnp.bfloat16)
    g_self2 = contract_rows(hidden_one, grad_before)
    g_nbr2 = contract_rows(pooled_two, grad_before)
    grad_hidden = contract_cols(grad_before, w_self2)
    grad_pooled = contract_cols(grad_before, w_nbr2).astype(jnp.bfloat16)
    grad_bordered = contract_rows(adjacency_two, grad_pooled) * fanout_inv
    return (g_self2, g_nbr2, grad_hidden, grad_bordered)


def backward_one(
    grad_hidden, before_one, self_rows, adjacency_one, pooled_one, slot_hot, w_self1, w_nbr1
):
    fanout_inv = 1.0 / FANOUT
    grad_before = (grad_hidden * swish_slope(before_one)).astype(jnp.bfloat16)
    g_one = contract_rows(jnp.concatenate([self_rows, pooled_one], axis=1), grad_before)
    grad_self_rows = contract_cols(grad_before, w_self1)
    grad_pooled = contract_cols(grad_before, w_nbr1).astype(jnp.bfloat16)
    upper = grad_self_rows.astype(jnp.bfloat16)
    lower = (grad_self_rows - upper.astype(jnp.float32)).astype(jnp.bfloat16)
    width = upper.shape[1]
    both = contract_rows(slot_hot, jnp.concatenate([upper, lower], axis=1))
    grad_fetched = both[:, :width] + both[:, width:] + contract_rows(adjacency_one, grad_pooled) * fanout_inv
    return (g_one, grad_fetched)


def trade_requests(wanted):
    return lax.all_to_all(wanted, ("grp", "dom"), split_axis=0, concat_axis=0, tiled=True)


def trade_rows(found):
    return lax.all_to_all(found, ("grp", "dom"), split_axis=0, concat_axis=0, tiled=True)


def tile_of(length, most):
    return most if length % most == 0 else length


def pick_kernel(index_ref, table_ref, found_ref, rounded):
    @pl.when(pl.program_id(0) == 0)
    def _():
        rounded[...] = table_ref[...].astype(jnp.bfloat16)

    lanes = lax.broadcasted_iota(jnp.int32, (index_ref.shape[0], table_ref.shape[0]), 1)
    chosen = jnp.where(index_ref[...] == lanes, 1.0, 0.0).astype(jnp.bfloat16)
    found_ref[...] = jnp.dot(chosen, rounded[...], preferred_element_type=jnp.float32).astype(
        jnp.bfloat16
    )


def pick_rows(index, table):
    count, (rows, width) = index.shape[0], table.shape
    tile = tile_of(count, 256)
    return pl.pallas_call(
        pick_kernel,
        grid=(count // tile,),
        out_shape=jax.ShapeDtypeStruct((count, width), jnp.bfloat16),
        in_specs=[
            pl.BlockSpec((tile, 1), lambda i: (i, 0)),
            pl.BlockSpec((rows, width), lambda i: (0, 0)),
        ],
        out_specs=pl.BlockSpec((tile, width), lambda i: (i, 0)),
        scratch_shapes=[pltpu.VMEM((rows, width), jnp.bfloat16)],
        compiler_params=pltpu.CompilerParams(vmem_limit_bytes=48 * 2**20),
        cost_estimate=pl.CostEstimate(
            flops=2 * count * rows * width, bytes_accessed=rows * width * 4, transcendentals=0
        ),
    )(index, table)


def update_tile(i, tile, index_ref, grads_ref, table_ref, accum_ref, new_table_ref, new_accum_ref):
    count = index_ref.shape[1]
    lanes = accum_ref.shape[1]
    start = pl.multiple_of(i * tile, tile)
    numbers = start + lax.broadcasted_iota(jnp.int32, (tile, count), 0)
    chosen = jnp.where(index_ref[...] == numbers, 1.0, 0.0).astype(jnp.bfloat16)
    grads = jnp.dot(
        chosen, grads_ref[...].reshape(count, -1), preferred_element_type=jnp.float32
    )
    means = jnp.mean(grads * grads, axis=1, keepdims=True)
    down = lax.broadcasted_iota(jnp.int32, (lanes, lanes), 0)
    across = lax.broadcasted_iota(jnp.int32, (lanes, lanes), 1)
    for j in range(tile // lanes):
        rows = pl.ds(pl.multiple_of(start + j * lanes, lanes), lanes)
        at = pl.ds(i * (tile // lanes) + j, 1)
        block = grads[j * lanes : (j + 1) * lanes]
        old = jnp.sum(jnp.where(down == across, accum_ref[at, :], 0.0), axis=1, keepdims=True)
        level = old + means[j * lanes : (j + 1) * lanes]
        new_accum_ref[at, :] = jnp.sum(
            jnp.where(down == across, level, 0.0), axis=0, keepdims=True
        )
        new_table_ref[rows, :] = table_ref[rows, :] - learning_rate * block / (
            jnp.sqrt(level) + epsilon
        )


def reduce_kernel(groups, domains, shares, *refs):
    parts = len(shares)
    x_refs, refs = refs[:parts], refs[parts:]
    grads_ref, index_ref, table_ref, accum_ref = refs[:4]
    out_refs, refs = refs[4 : 4 + parts], refs[4 + parts :]
    new_table_ref, new_accum_ref = refs[:2]
    acc, core_out, core_in, half_out, half_in, z_out, z_in, returned = refs[2:10]
    core_sem, half_sem, z_sem, trade_sem = refs[10:]
    xs = [x_refs[i].at[j] for i in range(parts) for j in range(shares[i])]
    outs = [out_refs[i].at[j] for i in range(parts) for j in range(shares[i])]
    chunks = len(xs)
    grp, dom = lax.axis_index("grp"), lax.axis_index("dom")
    core, layer = dom % 2, dom // 2
    layers = domains // 2
    bits = groups.bit_length() - 1
    half = groups * layers

    def other_grp(bit):
        mine = (grp // 2**bit) % 2
        return grp + (1 - 2 * mine) * 2**bit

    core_id = (grp, dom + 1 - 2 * core)
    half_ids = [(other_grp(bit), dom) for bit in range(bits)]
    layer_ids = [(grp, ((layer + d) % layers) * 2 + core) for d in range(1, layers)]
    devices = groups * domains
    me = grp * domains + dom

    def ahead(d):
        other = (me + d) % devices
        return other, (other // domains, other % domains)

    def each(count, body, first=0):
        def step(i, carry):
            body(i)
            return carry

        lax.fori_loop(first, count, step, 0)

    barrier = pltpu.get_barrier_semaphore()
    each(
        devices,
        lambda d: pl.semaphore_signal(
            barrier, inc=1, device_id=ahead(d)[1], device_id_type=pl.DeviceIdType.MESH
        ),
        1,
    )
    pl.semaphore_wait(barrier, devices - 1)

    def trade(d):
        other, target = ahead(d)
        return pltpu.make_async_remote_copy(
            src_ref=grads_ref.at[other],
            dst_ref=returned.at[me],
            send_sem=trade_sem.at[0, d],
            recv_sem=trade_sem.at[1, d],
            device_id=target,
            device_id_type=pl.DeviceIdType.MESH,
        )

    def send(source, target_ref, sems, target):
        copy = pltpu.make_async_remote_copy(
            src_ref=source,
            dst_ref=target_ref,
            send_sem=sems.at[0],
            recv_sem=sems.at[1],
            device_id=target,
            device_id_type=pl.DeviceIdType.MESH,
        )
        copy.start()
        return copy

    orders = [
        list(range(bits)) if k % 2 == 0 else list(range(bits))[::-1] for k in range(chunks)
    ]
    bit_of = lambda bit: (grp // 2**bit) % 2
    sent = []
    starts = []
    for k in range(chunks):
        at, size = core * half, half
        places = [at]
        for bit in orders[k]:
            size //= 2
            at = at + bit_of(bit) * size
            places.append(at)
        starts.append(places)

    def offset_of(step):
        return sum(half >> (i + 1) for i in range(step))

    copies = []
    for k in range(chunks):

        def narrow(i, k=k):
            core_out[k, i] = xs[k][(1 - core) * half + i].astype(jnp.bfloat16)

        each(half, narrow)
        copies.append(send(core_out.at[k], core_in.at[k], core_sem.at[0, k], core_id))
    sent += copies
    each(devices, lambda d: trade(d).start(), 1)
    returned[me] = grads_ref[me]

    for step in range(bits):
        later = []
        size = half >> (step + 1)
        slots = pl.ds(offset_of(step), size)
        for k in range(chunks):
            bit = orders[k][step]
            mine = bit_of(bit)
            base = starts[k][step] - starts[k][0]
            keep = base + mine * size
            give = base + (1 - mine) * size
            copies[k].wait_recv()

            def total(i, at, k=k, step=step):
                if step == 0:
                    return xs[k][core * half + at + i] + core_in[k, at + i].astype(jnp.float32)
                arrived = offset_of(step - 1) + at + i - base
                return acc[k, at + i] + half_in[k, arrived].astype(jnp.float32)

            def give_part(i, k=k, give=give, total=total, step=step):
                half_out[k, offset_of(step) + i] = total(i, give).astype(jnp.bfloat16)

            each(size, give_part)
            later.append(
                send(
                    half_out.at[k, slots],
                    half_in.at[k, slots],
                    half_sem.at[0, step, k],
                    half_ids[bit],
                )
            )

            def keep_part(i, k=k, keep=keep, total=total):
                acc[k, keep + i] = total(i, keep)

            each(size, keep_part)
        copies = later
        sent += copies

    z_copies = []
    for k in range(chunks):
        base = starts[k][bits] - starts[k][0]
        copies[k].wait_recv()
        last = offset_of(bits - 1)
        mine_now = []
        for d in range(1, layers):
            at = (layer + d) % layers
            z_out[k, d - 1] = (
                acc[k, base + at] + half_in[k, last + at].astype(jnp.float32)
            ).astype(jnp.bfloat16)
            mine_now.append(
                send(
                    z_out.at[k, d - 1],
                    z_in.at[k, d - 1],
                    z_sem.at[0, k, d - 1],
                    layer_ids[d - 1],
                )
            )
        z_copies.append(mine_now)
        sent += mine_now

    gathers = []
    for k in range(chunks):
        base = starts[k][bits] - starts[k][0]
        last = offset_of(bits - 1)
        value = acc[k, base + layer] + half_in[k, last + layer].astype(jnp.float32)
        for copy in z_copies[k]:
            copy.wait_recv()
        for d in range(1, layers):
            value = value + z_in[k, d - 1].astype(jnp.float32)
        at = starts[k][bits] + layer
        outs[k][at] = value.astype(jnp.bfloat16)
        mine_now = []
        for d in range(1, layers):
            mine_now.append(
                send(outs[k].at[at], outs[k].at[at], z_sem.at[1, k, d - 1], layer_ids[d - 1])
            )
        gathers.append(mine_now)
        sent += mine_now

    each(devices, lambda d: trade(d).wait_recv(), 1)
    tile = tile_of(table_ref.shape[0], 256)
    tiles = table_ref.shape[0] // tile
    turns = chunks * (bits + 1)

    def update(first, last):
        each(
            last,
            lambda i: update_tile(
                i, tile, index_ref, returned, table_ref, accum_ref, new_table_ref, new_accum_ref
            ),
            first,
        )

    turn = 0
    for step in reversed(range(bits)):
        later = []
        size = half >> (step + 1)
        for k in range(chunks):
            for copy in gathers[k]:
                copy.wait_recv()
            mine = pl.ds(starts[k][step + 1], size)
            later.append(
                [
                    send(
                        outs[k].at[mine],
                        outs[k].at[mine],
                        half_sem.at[1, step, k],
                        half_ids[orders[k][step]],
                    )
                ]
            )
            sent += later[-1]
            update(turn * tiles // turns, (turn + 1) * tiles // turns)
            turn += 1
        gathers = later
    last_copies = []
    for k in range(chunks):
        for copy in gathers[k]:
            copy.wait_recv()
        mine = pl.ds(starts[k][0], half)
        last_copies.append(
            send(outs[k].at[mine], outs[k].at[mine], core_sem.at[1, k], core_id)
        )
        update(turn * tiles // turns, (turn + 1) * tiles // turns)
        turn += 1
    for copy in last_copies:
        copy.wait_recv()
    for copy in sent + last_copies:
        copy.wait_send()
    each(devices, lambda d: trade(d).wait_send(), 1)


def sum_and_update(weight_grads, row_grads, incoming, table, accum, groups, domains):
    devices = groups * domains
    layers = domains // 2
    bits = groups.bit_length() - 1
    part = weight_grads[-1].size
    piece = 16
    width = part // (devices * piece)
    half = devices // 2
    unit = (piece, width)
    split = [g.reshape((g.size // part, devices) + unit) for g in weight_grads]
    chunks = sum(g.shape[0] for g in split)
    vmem = pl.BlockSpec(memory_space=pltpu.VMEM)
    lanes = 128
    size = sum(g.size for g in weight_grads)
    results = pl.pallas_call(
        functools.partial(reduce_kernel, groups, domains, tuple(g.shape[0] for g in split)),
        out_shape=[jax.ShapeDtypeStruct(g.shape, jnp.bfloat16) for g in split]
        + [
            jax.ShapeDtypeStruct(table.shape, jnp.float32),
            jax.ShapeDtypeStruct((table.shape[0] // lanes, lanes), jnp.float32),
        ],
        in_specs=[vmem] * (len(split) + 4),
        out_specs=[vmem] * (len(split) + 2),
        scratch_shapes=[
            pltpu.VMEM((chunks, half) + unit, jnp.float32),
            pltpu.VMEM((chunks, half) + unit, jnp.bfloat16),
            pltpu.VMEM((chunks, half) + unit, jnp.bfloat16),
            pltpu.VMEM((chunks, half) + unit, jnp.bfloat16),
            pltpu.VMEM((chunks, half) + unit, jnp.bfloat16),
            pltpu.VMEM((chunks, layers) + unit, jnp.bfloat16),
            pltpu.VMEM((chunks, layers) + unit, jnp.bfloat16),
            pltpu.VMEM(row_grads.shape, jnp.bfloat16),
            pltpu.SemaphoreType.DMA((2, chunks, 2)),
            pltpu.SemaphoreType.DMA((2, bits, chunks, 2)),
            pltpu.SemaphoreType.DMA((2, chunks, layers, 2)),
            pltpu.SemaphoreType.DMA((2, devices)),
        ],
        compiler_params=pltpu.CompilerParams(
            collective_id=0, has_side_effects=True, vmem_limit_bytes=60 * 2**20
        ),
        cost_estimate=pl.CostEstimate(
            flops=2 * row_grads.shape[0] * row_grads.shape[1] * table.size,
            bytes_accessed=6 * size + 8 * table.size,
            transcendentals=0,
        ),
    )(*split, row_grads, incoming.reshape(1, -1), table, accum.reshape(-1, lanes))
    sums = [r.reshape(g.shape) for r, g in zip(results, weight_grads)]
    return sums, results[-2], results[-1].reshape(-1)


def local(
    table,
    accum,
    w_self1,
    w_nbr1,
    w_self2,
    w_nbr2,
    fetch_owner,
    fetch_row,
    self_slot,
    nbr_one,
    nbr_two,
    cotangent,
):
    groups = lax.axis_size("grp")
    domains = lax.axis_size("dom")
    devices = groups * domains
    fetch_count = fetch_row.shape[0]
    capacity = max(2, 2 * fetch_count // devices)
    emb_width = table.shape[1]
    owners = fetch_owner[:, 0]
    owner_hot = hot(owners, devices)
    order = jnp.arange(fetch_count, dtype=jnp.int32)
    earlier = (order[:, None] > order[None, :]).astype(jnp.bfloat16)
    before = jnp.dot(earlier, owner_hot, preferred_element_type=jnp.float32)
    ranks = jnp.sum(before * owner_hot.astype(jnp.float32), axis=1).astype(jnp.int32)
    position = owners * capacity + ranks
    rank_hot = hot(ranks, capacity)
    digits = jnp.concatenate(
        [
            rank_hot * (fetch_row // 128).astype(jnp.bfloat16)[:, None],
            rank_hot * (fetch_row % 128).astype(jnp.bfloat16)[:, None],
        ],
        axis=1,
    )
    digits = contract_rows(owner_hot, digits)
    wanted = (digits[:, :capacity] * 128.0 + digits[:, capacity:]).astype(jnp.int32)
    place_hot = hot(position, devices * capacity)
    slot_hot = hot(self_slot, fetch_count)
    incoming = trade_requests(wanted)
    found = pick_rows(incoming.reshape(-1, 1), table).reshape(devices, capacity, emb_width)
    replies = trade_rows(found)
    fetched = jnp.dot(
        place_hot,
        replies.reshape(devices * capacity, emb_width),
        preferred_element_type=jnp.float32,
    ).astype(jnp.bfloat16)
    self_rows, adjacency_one, pooled_one, before_one = forward_one(
        fetched, slot_hot, nbr_one, w_self1, w_nbr1
    )
    hidden_one = jax.nn.silu(before_one).astype(jnp.bfloat16)
    nodes = hidden_one.shape[0]
    bordered = with_halo(hidden_one, ((("grp", "dom"), 0),), BORDER)
    adjacency_two, pooled_two, before_two, normed, scale = forward_two(
        hidden_one, bordered, nbr_two, w_self2, w_nbr2
    )
    embedded = normed.astype(jnp.bfloat16)
    g_self2, g_nbr2, grad_hidden, grad_bordered = backward_two(
        cotangent, hidden_one, adjacency_two, pooled_two, before_two, normed, scale, w_self2, w_nbr2
    )
    middle = grad_hidden + grad_bordered[BORDER : BORDER + nodes]
    edges = jnp.concatenate([grad_bordered[:BORDER], grad_bordered[BORDER + nodes :]], axis=0)
    arrived = with_halo(edges, ((("grp", "dom"), 0),), BORDER)
    grad_hidden = (
        middle.at[:BORDER]
        .add(arrived[:BORDER])
        .at[nodes - BORDER :]
        .add(arrived[arrived.shape[0] - BORDER :])
    )
    g_one, grad_fetched = backward_one(
        grad_hidden, before_one, self_rows, adjacency_one, pooled_one, slot_hot, w_self1, w_nbr1
    )
    grad_buffer = (
        contract_rows(place_hot, grad_fetched.astype(jnp.bfloat16))
        .astype(jnp.bfloat16)
        .reshape(devices, capacity, emb_width)
    )
    sums, new_table, new_accum = sum_and_update(
        (g_self2, g_nbr2, g_one), grad_buffer, incoming, table, accum, groups, domains
    )
    sum_self2, sum_nbr2, sum_one = sums
    sum_self1, sum_nbr1 = sum_one[:emb_width], sum_one[emb_width:]
    return (embedded, new_table, new_accum, sum_self1, sum_nbr1, sum_self2, sum_nbr2)


def solution(mesh):
    in_specs = (
        P(("grp", "dom"), None),
        P(("grp", "dom")),
        P(),
        P(),
        P(),
        P(),
        P(("grp", "dom"), None),
        P(("grp", "dom")),
        P(("grp", "dom")),
        P(("grp", "dom"), None),
        P(("grp", "dom"), None),
        P(("grp", "dom"), None),
    )
    out_specs = (
        P(("grp", "dom"), None),
        P(("grp", "dom"), None),
        P(("grp", "dom")),
        P(),
        P(),
        P(),
        P(),
    )
    return jax.shard_map(local, mesh=mesh, in_specs=in_specs, out_specs=out_specs, check_vma=False)
```

```python
import functools

import jax
import jax.numpy as jnp
from jax import lax
from jax.experimental import pallas as pl
from jax.experimental.pallas import tpu as pltpu
from jax.sharding import PartitionSpec as P

FANOUT = 8
BORDER = 64


epsilon = 1e-06
learning_rate = 0.1


def with_halo(x, sides, width):
    for axis, dim in sides:
        devices, length = (lax.axis_size(axis), x.shape[dim])
        up = [(i, (i + 1) % devices) for i in range(devices)]
        down = [(j, i) for i, j in up]
        last = lax.slice_in_dim(x, length - width, length, axis=dim)
        leading = lax.slice_in_dim(x, 0, width, axis=dim)
        before = lax.ppermute(last, axis, up)
        after = lax.ppermute(leading, axis, down)
        x = jnp.concatenate([before, x, after], axis=dim)
    return x


def swish_slope(values):
    logistic = jax.nn.sigmoid(values)
    return logistic + values * logistic * (1.0 - logistic)


def hot(index, width):
    return (index[:, None] == jnp.arange(width, dtype=jnp.int32)[None, :]).astype(jnp.bfloat16)


def contract_rows(left, right):
    return lax.dot_general(
        left, right, (((0,), (0,)), ((), ())), preferred_element_type=jnp.float32
    )


def contract_cols(left, right):
    return lax.dot_general(
        left, right, (((1,), (1,)), ((), ())), preferred_element_type=jnp.float32
    )


def forward_one(fetched, slot_hot, adjacency_one, w_self1, w_nbr1):
    fanout = FANOUT
    self_rows = jnp.dot(
        slot_hot, fetched, preferred_element_type=jnp.float32
    ).astype(jnp.bfloat16)
    pooled_one = (
        jnp.dot(adjacency_one, fetched, preferred_element_type=jnp.float32) / fanout
    ).astype(jnp.bfloat16)
    before_one = jnp.dot(self_rows, w_self1, preferred_element_type=jnp.float32) + jnp.dot(
        pooled_one, w_nbr1, preferred_element_type=jnp.float32
    )
    return (self_rows, pooled_one, before_one)


def forward_two(hidden_one, bordered, adjacency_two, w_self2, w_nbr2):
    fanout = FANOUT
    pooled_two = (
        jnp.dot(adjacency_two, bordered, preferred_element_type=jnp.float32) / fanout
    ).astype(jnp.bfloat16)
    before_two = jnp.dot(hidden_one, w_self2, preferred_element_type=jnp.float32) + jnp.dot(
        pooled_two, w_nbr2, preferred_element_type=jnp.float32
    )
    lifted = jax.nn.silu(before_two)
    scale = lax.rsqrt(jnp.mean(lifted * lifted, axis=1, keepdims=True) + epsilon)
    return (pooled_two, before_two, lifted * scale, scale)


def backward_two(
    upstream, hidden_one, adjacency_two, pooled_two, before_two, normed, scale, w_self2, w_nbr2
):
    fanout_inv = 1.0 / FANOUT
    grad_lifted = scale * (upstream - normed * jnp.mean(upstream * normed, axis=1, keepdims=True))
    grad_before = (grad_lifted * swish_slope(before_two)).astype(jnp.bfloat16)
    g_self2 = contract_rows(hidden_one, grad_before)
    g_nbr2 = contract_rows(pooled_two, grad_before)
    grad_hidden = contract_cols(grad_before, w_self2)
    grad_pooled = contract_cols(grad_before, w_nbr2).astype(jnp.bfloat16)
    grad_bordered = contract_rows(adjacency_two, grad_pooled) * fanout_inv
    return (g_self2, g_nbr2, grad_hidden, grad_bordered)


def backward_one(
    grad_hidden, before_one, self_rows, adjacency_one, pooled_one, slot_hot, w_self1, w_nbr1
):
    fanout_inv = 1.0 / FANOUT
    grad_before = (grad_hidden * swish_slope(before_one)).astype(jnp.bfloat16)
    g_one = contract_rows(jnp.concatenate([self_rows, pooled_one], axis=1), grad_before)
    grad_self_rows = contract_cols(grad_before, w_self1)
    grad_pooled = contract_cols(grad_before, w_nbr1).astype(jnp.bfloat16)
    upper = grad_self_rows.astype(jnp.bfloat16)
    lower = (grad_self_rows - upper.astype(jnp.float32)).astype(jnp.bfloat16)
    width = upper.shape[1]
    both = contract_rows(slot_hot, jnp.concatenate([upper, lower], axis=1))
    grad_fetched = both[:, :width] + both[:, width:] + contract_rows(adjacency_one, grad_pooled) * fanout_inv
    return (g_one, grad_fetched)


def tile_of(length, most):
    return most if length % most == 0 else length


def count_rows(i, tile, neighbours_ref, out_ref):
    rows = pl.ds(pl.multiple_of(i * tile, tile), tile)
    near = neighbours_ref[rows, :]
    lanes = lax.broadcasted_iota(jnp.int32, (tile, out_ref.shape[1]), 1)
    total = jnp.zeros((tile, out_ref.shape[1]), jnp.float32)
    for k in range(near.shape[1]):
        total = total + jnp.where(near[:, k : k + 1] == lanes, 1.0, 0.0)
    out_ref[rows, :] = total.astype(jnp.bfloat16)


def fetch_kernel(
    groups,
    domains,
    batch,
    wanted_ref,
    table_ref,
    one_ref,
    two_ref,
    replies_ref,
    incoming_ref,
    count_one_ref,
    count_two_ref,
    rounded,
    found,
    chosen,
    ask_sem,
    reply_sem,
):
    grp, dom = lax.axis_index("grp"), lax.axis_index("dom")
    devices = groups * domains
    me = grp * domains + dom
    capacity = replies_ref.shape[1]
    lanes = wanted_ref.shape[2]

    def place(other):
        return (other // domains, other % domains)

    def each(first, last, body):
        def step(i, carry):
            body(i)
            return carry

        lax.fori_loop(first, last, step, 0)

    barrier = pltpu.get_barrier_semaphore()
    each(
        1,
        devices,
        lambda d: pl.semaphore_signal(
            barrier,
            inc=1,
            device_id=place((me + d) % devices),
            device_id_type=pl.DeviceIdType.MESH,
        ),
    )
    pl.semaphore_wait(barrier, devices - 1)

    def ask(d):
        other = (me + d) % devices
        return pltpu.make_async_remote_copy(
            src_ref=wanted_ref.at[other],
            dst_ref=incoming_ref.at[me],
            send_sem=ask_sem.at[0, d],
            recv_sem=ask_sem.at[1, d],
            device_id=place(other),
            device_id_type=pl.DeviceIdType.MESH,
        )

    def reply(d):
        other = (me + devices - d) % devices
        return pltpu.make_async_remote_copy(
            src_ref=found.at[other],
            dst_ref=replies_ref.at[me],
            send_sem=reply_sem.at[0, d],
            recv_sem=reply_sem.at[1, d],
            device_id=place(other),
            device_id_type=pl.DeviceIdType.MESH,
        )

    each(1, devices, lambda d: ask(d).start())
    incoming_ref[me] = wanted_ref[me]
    rounded[...] = table_ref[...].astype(jnp.bfloat16)
    down = lax.broadcasted_iota(jnp.int32, (capacity, lanes), 0)
    across = lax.broadcasted_iota(jnp.int32, (capacity, lanes), 1)

    def pick(first):
        for q in range(batch):
            source = (me + 2 * devices - first - q) % devices
            listed = incoming_ref[source][0:1, :].astype(jnp.float32)
            column = jnp.sum(jnp.where(down == across, listed, 0.0), axis=1, keepdims=True)
            numbers = lax.broadcasted_iota(jnp.int32, (capacity, table_ref.shape[0]), 1)
            chosen[q * capacity : (q + 1) * capacity, :] = jnp.where(
                column.astype(jnp.int32) == numbers, 1.0, 0.0
            ).astype(jnp.bfloat16)
        rows = jnp.dot(chosen[...], rounded[...], preferred_element_type=jnp.float32).astype(
            jnp.bfloat16
        )
        for q in range(batch):
            source = (me + 2 * devices - first - q) % devices
            found[source] = rows[q * capacity : (q + 1) * capacity]

    def turn(j):
        first = 1 + j * batch
        for q in range(batch):
            ask(first + q).wait_recv()
        pick(first)
        for q in range(batch):
            reply(first + q).start()

    turns = devices // batch
    each(0, turns - 1, turn)
    first = 1 + (turns - 1) * batch
    for q in range(batch - 1):
        ask(first + q).wait_recv()
    pick(first)
    for q in range(batch - 1):
        reply(first + q).start()
    replies_ref[me] = found[me]
    tile = 16
    each(0, one_ref.shape[0] // tile, lambda i: count_rows(i, tile, one_ref, count_one_ref))
    each(0, two_ref.shape[0] // tile, lambda i: count_rows(i, tile, two_ref, count_two_ref))
    each(1, devices, lambda d: reply(d).wait_recv())
    each(1, devices, lambda d: ask(d).wait_send())
    each(1, devices, lambda d: reply(d).wait_send())


def fetch(wanted, table, nbr_one, nbr_two, fetch_count, groups, domains):
    devices, capacity = wanted.shape
    rows, width = table.shape
    nodes = nbr_one.shape[0]
    lanes = 128
    batch = 4
    padded = jnp.broadcast_to(
        jnp.pad(wanted, ((0, 0), (0, lanes - capacity)))[:, None, :], (devices, 8, lanes)
    )
    vmem = pl.BlockSpec(memory_space=pltpu.VMEM)
    replies, incoming, one, two = pl.pallas_call(
        functools.partial(fetch_kernel, groups, domains, batch),
        out_shape=[
            jax.ShapeDtypeStruct((devices, capacity, width), jnp.bfloat16),
            jax.ShapeDtypeStruct((devices, 8, lanes), jnp.int32),
            jax.ShapeDtypeStruct((nodes, fetch_count), jnp.bfloat16),
            jax.ShapeDtypeStruct((nodes, nodes + 2 * BORDER), jnp.bfloat16),
        ],
        in_specs=[vmem] * 4,
        out_specs=[vmem] * 4,
        scratch_shapes=[
            pltpu.VMEM((rows, width), jnp.bfloat16),
            pltpu.VMEM((devices, capacity, width), jnp.bfloat16),
            pltpu.VMEM((batch * capacity, rows), jnp.bfloat16),
            pltpu.SemaphoreType.DMA((2, devices)),
            pltpu.SemaphoreType.DMA((2, devices)),
        ],
        compiler_params=pltpu.CompilerParams(
            collective_id=1, has_side_effects=True, vmem_limit_bytes=48 * 2**20
        ),
        cost_estimate=pl.CostEstimate(
            flops=2 * devices * capacity * rows * width,
            bytes_accessed=rows * width * 4,
            transcendentals=0,
        ),
    )(padded, table, nbr_one, nbr_two)
    return replies, incoming[:, 0, :capacity], one, two


def update_tile(i, tile, index_ref, grads_ref, table_ref, accum_ref, new_table_ref, new_accum_ref):
    count = index_ref.shape[1]
    lanes = accum_ref.shape[1]
    start = pl.multiple_of(i * tile, tile)
    numbers = start + lax.broadcasted_iota(jnp.int32, (tile, count), 0)
    chosen = jnp.where(index_ref[...] == numbers, 1.0, 0.0).astype(jnp.bfloat16)
    grads = jnp.dot(
        chosen, grads_ref[...].reshape(count, -1), preferred_element_type=jnp.float32
    )
    means = jnp.mean(grads * grads, axis=1, keepdims=True)
    down = lax.broadcasted_iota(jnp.int32, (lanes, lanes), 0)
    across = lax.broadcasted_iota(jnp.int32, (lanes, lanes), 1)
    for j in range(tile // lanes):
        rows = pl.ds(pl.multiple_of(start + j * lanes, lanes), lanes)
        at = pl.ds(i * (tile // lanes) + j, 1)
        block = grads[j * lanes : (j + 1) * lanes]
        old = jnp.sum(jnp.where(down == across, accum_ref[at, :], 0.0), axis=1, keepdims=True)
        level = old + means[j * lanes : (j + 1) * lanes]
        new_accum_ref[at, :] = jnp.sum(
            jnp.where(down == across, level, 0.0), axis=0, keepdims=True
        )
        new_table_ref[rows, :] = table_ref[rows, :] - learning_rate * block / (
            jnp.sqrt(level) + epsilon
        )


def reduce_kernel(groups, domains, shares, *refs):
    parts = len(shares)
    x_refs, refs = refs[:parts], refs[parts:]
    grads_ref, index_ref, table_ref, accum_ref = refs[:4]
    out_refs, refs = refs[4 : 4 + parts], refs[4 + parts :]
    new_table_ref, new_accum_ref = refs[:2]
    acc, core_out, core_in, half_out, half_in, z_out, z_in, returned = refs[2:10]
    core_sem, half_sem, z_sem, trade_sem = refs[10:]
    xs = [x_refs[i].at[j] for i in range(parts) for j in range(shares[i])]
    outs = [out_refs[i].at[j] for i in range(parts) for j in range(shares[i])]
    chunks = len(xs)
    grp, dom = lax.axis_index("grp"), lax.axis_index("dom")
    core, layer = dom % 2, dom // 2
    layers = domains // 2
    bits = groups.bit_length() - 1
    half = groups * layers

    def other_grp(bit):
        mine = (grp // 2**bit) % 2
        return grp + (1 - 2 * mine) * 2**bit

    core_id = (grp, dom + 1 - 2 * core)
    half_ids = [(other_grp(bit), dom) for bit in range(bits)]
    layer_ids = [(grp, ((layer + d) % layers) * 2 + core) for d in range(1, layers)]
    devices = groups * domains
    me = grp * domains + dom

    def ahead(d):
        other = (me + d) % devices
        return other, (other // domains, other % domains)

    def each(count, body, first=0):
        def step(i, carry):
            body(i)
            return carry

        lax.fori_loop(first, count, step, 0)

    barrier = pltpu.get_barrier_semaphore()
    each(
        devices,
        lambda d: pl.semaphore_signal(
            barrier, inc=1, device_id=ahead(d)[1], device_id_type=pl.DeviceIdType.MESH
        ),
        1,
    )
    pl.semaphore_wait(barrier, devices - 1)

    def trade(d):
        other, target = ahead(d)
        return pltpu.make_async_remote_copy(
            src_ref=grads_ref.at[other],
            dst_ref=returned.at[me],
            send_sem=trade_sem.at[0, d],
            recv_sem=trade_sem.at[1, d],
            device_id=target,
            device_id_type=pl.DeviceIdType.MESH,
        )

    def send(source, target_ref, sems, target):
        copy = pltpu.make_async_remote_copy(
            src_ref=source,
            dst_ref=target_ref,
            send_sem=sems.at[0],
            recv_sem=sems.at[1],
            device_id=target,
            device_id_type=pl.DeviceIdType.MESH,
        )
        copy.start()
        return copy

    orders = [
        list(range(bits)) if k % 2 == 0 else list(range(bits))[::-1] for k in range(chunks)
    ]
    bit_of = lambda bit: (grp // 2**bit) % 2
    sent = []
    starts = []
    for k in range(chunks):
        at, size = core * half, half
        places = [at]
        for bit in orders[k]:
            size //= 2
            at = at + bit_of(bit) * size
            places.append(at)
        starts.append(places)

    def offset_of(step):
        return sum(half >> (i + 1) for i in range(step))

    copies = []
    for k in range(chunks):

        def narrow(i, k=k):
            core_out[k, i] = xs[k][(1 - core) * half + i].astype(jnp.bfloat16)

        each(half, narrow)
        copies.append(send(core_out.at[k], core_in.at[k], core_sem.at[0, k], core_id))
    sent += copies
    each(devices, lambda d: trade(d).start(), 1)
    returned[me] = grads_ref[me]

    for step in range(bits):
        later = []
        size = half >> (step + 1)
        slots = pl.ds(offset_of(step), size)
        for k in range(chunks):
            bit = orders[k][step]
            mine = bit_of(bit)
            base = starts[k][step] - starts[k][0]
            keep = base + mine * size
            give = base + (1 - mine) * size
            copies[k].wait_recv()

            def total(i, at, k=k, step=step):
                if step == 0:
                    return xs[k][core * half + at + i] + core_in[k, at + i].astype(jnp.float32)
                arrived = offset_of(step - 1) + at + i - base
                return acc[k, at + i] + half_in[k, arrived].astype(jnp.float32)

            def give_part(i, k=k, give=give, total=total, step=step):
                half_out[k, offset_of(step) + i] = total(i, give).astype(jnp.bfloat16)

            each(size, give_part)
            later.append(
                send(
                    half_out.at[k, slots],
                    half_in.at[k, slots],
                    half_sem.at[0, step, k],
                    half_ids[bit],
                )
            )

            def keep_part(i, k=k, keep=keep, total=total):
                acc[k, keep + i] = total(i, keep)

            each(size, keep_part)
        copies = later
        sent += copies

    z_copies = []
    for k in range(chunks):
        base = starts[k][bits] - starts[k][0]
        copies[k].wait_recv()
        last = offset_of(bits - 1)
        mine_now = []
        for d in range(1, layers):
            at = (layer + d) % layers
            z_out[k, d - 1] = (
                acc[k, base + at] + half_in[k, last + at].astype(jnp.float32)
            ).astype(jnp.bfloat16)
            mine_now.append(
                send(
                    z_out.at[k, d - 1],
                    z_in.at[k, d - 1],
                    z_sem.at[0, k, d - 1],
                    layer_ids[d - 1],
                )
            )
        z_copies.append(mine_now)
        sent += mine_now

    gathers = []
    for k in range(chunks):
        base = starts[k][bits] - starts[k][0]
        last = offset_of(bits - 1)
        value = acc[k, base + layer] + half_in[k, last + layer].astype(jnp.float32)
        for copy in z_copies[k]:
            copy.wait_recv()
        for d in range(1, layers):
            value = value + z_in[k, d - 1].astype(jnp.float32)
        at = starts[k][bits] + layer
        outs[k][at] = value.astype(jnp.bfloat16)
        mine_now = []
        for d in range(1, layers):
            mine_now.append(
                send(outs[k].at[at], outs[k].at[at], z_sem.at[1, k, d - 1], layer_ids[d - 1])
            )
        gathers.append(mine_now)
        sent += mine_now

    each(devices, lambda d: trade(d).wait_recv(), 1)
    tile = tile_of(table_ref.shape[0], 256)
    tiles = table_ref.shape[0] // tile
    turns = chunks * (bits + 1)

    def update(first, last):
        each(
            last,
            lambda i: update_tile(
                i, tile, index_ref, returned, table_ref, accum_ref, new_table_ref, new_accum_ref
            ),
            first,
        )

    turn = 0
    for step in reversed(range(bits)):
        later = []
        size = half >> (step + 1)
        for k in range(chunks):
            for copy in gathers[k]:
                copy.wait_recv()
            mine = pl.ds(starts[k][step + 1], size)
            later.append(
                [
                    send(
                        outs[k].at[mine],
                        outs[k].at[mine],
                        half_sem.at[1, step, k],
                        half_ids[orders[k][step]],
                    )
                ]
            )
            sent += later[-1]
            update(turn * tiles // turns, (turn + 1) * tiles // turns)
            turn += 1
        gathers = later
    last_copies = []
    for k in range(chunks):
        for copy in gathers[k]:
            copy.wait_recv()
        mine = pl.ds(starts[k][0], half)
        last_copies.append(
            send(outs[k].at[mine], outs[k].at[mine], core_sem.at[1, k], core_id)
        )
        update(turn * tiles // turns, (turn + 1) * tiles // turns)
        turn += 1
    for copy in last_copies:
        copy.wait_recv()
    for copy in sent + last_copies:
        copy.wait_send()
    each(devices, lambda d: trade(d).wait_send(), 1)


def sum_and_update(weight_grads, row_grads, incoming, table, accum, groups, domains):
    devices = groups * domains
    layers = domains // 2
    bits = groups.bit_length() - 1
    part = weight_grads[-1].size
    piece = 16
    width = part // (devices * piece)
    half = devices // 2
    unit = (piece, width)
    split = [g.reshape((g.size // part, devices) + unit) for g in weight_grads]
    chunks = sum(g.shape[0] for g in split)
    vmem = pl.BlockSpec(memory_space=pltpu.VMEM)
    lanes = 128
    size = sum(g.size for g in weight_grads)
    results = pl.pallas_call(
        functools.partial(reduce_kernel, groups, domains, tuple(g.shape[0] for g in split)),
        out_shape=[jax.ShapeDtypeStruct(g.shape, jnp.bfloat16) for g in split]
        + [
            jax.ShapeDtypeStruct(table.shape, jnp.float32),
            jax.ShapeDtypeStruct((table.shape[0] // lanes, lanes), jnp.float32),
        ],
        in_specs=[vmem] * (len(split) + 4),
        out_specs=[vmem] * (len(split) + 2),
        scratch_shapes=[
            pltpu.VMEM((chunks, half) + unit, jnp.float32),
            pltpu.VMEM((chunks, half) + unit, jnp.bfloat16),
            pltpu.VMEM((chunks, half) + unit, jnp.bfloat16),
            pltpu.VMEM((chunks, half) + unit, jnp.bfloat16),
            pltpu.VMEM((chunks, half) + unit, jnp.bfloat16),
            pltpu.VMEM((chunks, layers) + unit, jnp.bfloat16),
            pltpu.VMEM((chunks, layers) + unit, jnp.bfloat16),
            pltpu.VMEM(row_grads.shape, jnp.bfloat16),
            pltpu.SemaphoreType.DMA((2, chunks, 2)),
            pltpu.SemaphoreType.DMA((2, bits, chunks, 2)),
            pltpu.SemaphoreType.DMA((2, chunks, layers, 2)),
            pltpu.SemaphoreType.DMA((2, devices)),
        ],
        compiler_params=pltpu.CompilerParams(
            collective_id=0, has_side_effects=True, vmem_limit_bytes=60 * 2**20
        ),
        cost_estimate=pl.CostEstimate(
            flops=2 * row_grads.shape[0] * row_grads.shape[1] * table.size,
            bytes_accessed=6 * size + 8 * table.size,
            transcendentals=0,
        ),
    )(*split, row_grads, incoming.reshape(1, -1), table, accum.reshape(-1, lanes))
    sums = [r.reshape(g.shape) for r, g in zip(results, weight_grads)]
    return sums, results[-2], results[-1].reshape(-1)


def local(
    table,
    accum,
    w_self1,
    w_nbr1,
    w_self2,
    w_nbr2,
    fetch_owner,
    fetch_row,
    self_slot,
    nbr_one,
    nbr_two,
    cotangent,
):
    groups = lax.axis_size("grp")
    domains = lax.axis_size("dom")
    devices = groups * domains
    fetch_count = fetch_row.shape[0]
    capacity = max(2, 2 * fetch_count // devices)
    emb_width = table.shape[1]
    owners = fetch_owner[:, 0]
    owner_hot = hot(owners, devices)
    order = jnp.arange(fetch_count, dtype=jnp.int32)
    earlier = (order[:, None] > order[None, :]).astype(jnp.bfloat16)
    before = jnp.dot(earlier, owner_hot, preferred_element_type=jnp.float32)
    ranks = jnp.sum(before * owner_hot.astype(jnp.float32), axis=1).astype(jnp.int32)
    position = owners * capacity + ranks
    rank_hot = hot(ranks, capacity)
    digits = jnp.concatenate(
        [
            rank_hot * (fetch_row // 128).astype(jnp.bfloat16)[:, None],
            rank_hot * (fetch_row % 128).astype(jnp.bfloat16)[:, None],
        ],
        axis=1,
    )
    digits = contract_rows(owner_hot, digits)
    wanted = (digits[:, :capacity] * 128.0 + digits[:, capacity:]).astype(jnp.int32)
    place_hot = hot(position, devices * capacity)
    slot_hot = hot(self_slot, fetch_count)
    replies, incoming, adjacency_one, adjacency_two = fetch(
        wanted, table, nbr_one, nbr_two, fetch_count, groups, domains
    )
    fetched = jnp.dot(
        place_hot,
        replies.reshape(devices * capacity, emb_width),
        preferred_element_type=jnp.float32,
    ).astype(jnp.bfloat16)
    self_rows, pooled_one, before_one = forward_one(
        fetched, slot_hot, adjacency_one, w_self1, w_nbr1
    )
    hidden_one = jax.nn.silu(before_one).astype(jnp.bfloat16)
    nodes = hidden_one.shape[0]
    bordered = with_halo(hidden_one, ((("grp", "dom"), 0),), BORDER)
    pooled_two, before_two, normed, scale = forward_two(
        hidden_one, bordered, adjacency_two, w_self2, w_nbr2
    )
    embedded = normed.astype(jnp.bfloat16)
    g_self2, g_nbr2, grad_hidden, grad_bordered = backward_two(
        cotangent, hidden_one, adjacency_two, pooled_two, before_two, normed, scale, w_self2, w_nbr2
    )
    middle = grad_hidden + grad_bordered[BORDER : BORDER + nodes]
    edges = jnp.concatenate([grad_bordered[:BORDER], grad_bordered[BORDER + nodes :]], axis=0)
    arrived = with_halo(edges, ((("grp", "dom"), 0),), BORDER)
    grad_hidden = (
        middle.at[:BORDER]
        .add(arrived[:BORDER])
        .at[nodes - BORDER :]
        .add(arrived[arrived.shape[0] - BORDER :])
    )
    g_one, grad_fetched = backward_one(
        grad_hidden, before_one, self_rows, adjacency_one, pooled_one, slot_hot, w_self1, w_nbr1
    )
    grad_buffer = (
        contract_rows(place_hot, grad_fetched.astype(jnp.bfloat16))
        .astype(jnp.bfloat16)
        .reshape(devices, capacity, emb_width)
    )
    sums, new_table, new_accum = sum_and_update(
        (g_self2, g_nbr2, g_one), grad_buffer, incoming, table, accum, groups, domains
    )
    sum_self2, sum_nbr2, sum_one = sums
    sum_self1, sum_nbr1 = sum_one[:emb_width], sum_one[emb_width:]
    return (embedded, new_table, new_accum, sum_self1, sum_nbr1, sum_self2, sum_nbr2)


def solution(mesh):
    in_specs = (
        P(("grp", "dom"), None),
        P(("grp", "dom")),
        P(),
        P(),
        P(),
        P(),
        P(("grp", "dom"), None),
        P(("grp", "dom")),
        P(("grp", "dom")),
        P(("grp", "dom"), None),
        P(("grp", "dom"), None),
        P(("grp", "dom"), None),
    )
    out_specs = (
        P(("grp", "dom"), None),
        P(("grp", "dom"), None),
        P(("grp", "dom")),
        P(),
        P(),
        P(),
        P(),
    )
    return jax.shard_map(local, mesh=mesh, in_specs=in_specs, out_specs=out_specs, check_vma=False)
```
